32 devices in a mesh: groups: 2 (over x), ep: 4 (over y, core), col: 4 (over z).
Axes of the slice: x: 2, y: 2, z: 4, core: 2. Of those that a mesh axis runs over, the one named last changes fastest.
Arguments:
- tokens: bfloat16 [512, 4096], P(('groups', 'ep', 'col')), parts along dimension 0, may hold values from -6 to 6
- expert_ids: int32 [512, 8], P(('groups', 'ep', 'col')), parts along dimension 0, may hold values from 0 to 15, all different within a row; in each aligned block of 16 rows (0 to 15, 16 to 31, ...) at most 12 rows name the same one
- gate_weights: bfloat16 [512, 8], P(('groups', 'ep', 'col')), parts along dimension 0, may hold values from 0.099609375 to 0.5
- mix_coef: float32 [16, 2, 16], P('ep'), may hold values from -0.5 to 0.5
- factor_in: bfloat16 [16, 2, 4096, 256], P(('ep', 'col')), may hold values from -0.09375 to 0.09375
- factor_out: bfloat16 [16, 768, 256], P(('ep', 'col')), may hold values from -0.21875 to 0.21875
- basis_in: bfloat16 [16, 256, 1536], P(None, None, 'col'), may hold values from -0.375 to 0.375
- basis_out: bfloat16 [16, 256, 4096], P(None, None, 'col'), may hold values from -0.375 to 0.375
Outputs:
- moe_out: bfloat16 [512, 4096], P(('groups', 'ep', 'col')), parts along dimension 0
The draws below stay inside these ranges and needn't reach their ends.
There are 2 independent parts, one for each index of `groups`. The reference program is written for one: setup_inputs(seed, part) draws one part's arguments, and reference() takes and returns one part's arrays. A program takes and returns all parts, laid end to end along the dimension named above; an argument that names none is the same for every part. Nothing has to cross between parts.
Inputs may be any that keep to these rules, and one draw needn't show every extreme that they name: `expert_ids`: each token names 8 different experts; among the 16 tokens of one device (aligned blocks of 16 rows) no expert is named by more than 12 tokens, a bound that some block reaches.
All inputs are finite; a program needn't handle non-finite values.
Results may differ from the reference program's by a relative error of at most 0.0092.
Values may be sent and summed in bfloat16 or wider, within the bound.
A program may use at most 64 MiB of HBM per device.

```python
import math
import jax
import jax.numpy as jnp
import numpy as np
from jax import lax

D = 4096
FF = 768
RANK = 256
BASES = 16
TOPK = 8
TOK_DEV = 16
EXPERTS = 16
TOKENS = 256
CAP = 12


def steps_of(stream_key, extent, cuts, least, high):
    loudness, own = 1.0, jax.random.fold_in(stream_key, 6)
    for axis_at, shards_of in cuts:
        heights = jnp.exp(jax.random.uniform(jax.random.fold_in(own, axis_at), (shards_of,), jnp.float32, least / len(cuts), high / len(cuts)))
        loudness = loudness * jnp.repeat(heights, extent[axis_at] // shards_of).reshape([-1 if axis == axis_at else 1 for axis in range(len(extent))])
    return loudness


def routed_block(stream_key, own, number, rows, number_of, top, most, slope):
    sequence = jax.random.permutation(stream_key, number_of)
    heavy_load, usual = shares(number_of, rows * top, most, slope, True), shares(number_of, rows * top, most, slope, False)
    places = jnp.arange(number_of)

    def named(lengths, turn):
        used = int((lengths > 0).sum())
        fixed = max(1, used // 4)
        moved = fixed + (places - fixed + turn * (used - fixed)) % max(1, number_of - fixed)
        return jnp.zeros((number_of,), jnp.int32).at[sequence[jnp.where(places < fixed, places, moved)]].set(jnp.asarray(lengths, jnp.int32))

    lengths = jnp.where(number % 4 == 0, named(heavy_load, number // 4), named(usual, number - number // 4 - 1))
    mixed = jax.random.permutation(jax.random.fold_in(own, 3), number_of)
    source_of, sink = mixed[0:number_of // 2 * 2:2], mixed[1:number_of // 2 * 2:2]
    margin = jnp.minimum(lengths[source_of] - 1, most - lengths[sink]) // 2
    margin = jnp.where((source_of == sequence[0]) | (sink == sequence[0]) | (lengths[sink] == 0), 0, jnp.maximum(margin, 0))
    moved = jax.random.randint(jax.random.fold_in(own, 4), (number_of // 2,), 0, 1 << 20) % (margin + 1)
    lengths = lengths.at[source_of].add(-moved).at[sink].add(moved)
    items = jnp.searchsorted(jnp.cumsum(lengths), jnp.arange(rows * top), side="right").astype(jnp.int32)
    grid = items.reshape(top, rows).T
    grid = grid[jax.random.permutation(jax.random.fold_in(own, 1), rows)]
    turn = jax.random.randint(jax.random.fold_in(own, 2), (rows, 1), 0, top)
    return jnp.take_along_axis(grid, (jnp.arange(top)[None, :] + turn) % top, axis=1)


def shares(amount, total, reach, lean, full):
    portions = [(1 << 20) // math.isqrt(rank ** lean) + 1 for rank in range(1, amount + 1)]
    largest = reach if full else min(reach, max(-(-total // amount), total * portions[0] // sum(portions)))
    least = 1 if total - largest >= amount - 1 else 0
    holding, spare = [largest] + [least] * (amount - 1), total - largest - least * (amount - 1)
    while spare > 0:
        movable = [i for i in range(1, amount) if holding[i] < largest] or [i for i in range(1, amount) if holding[i] < reach]
        pool, left = sum([portions[i] for i in movable]), spare
        for i in movable:
            addition = min(reach - holding[i], max(1, left * portions[i] // pool), spare)
            holding[i] = holding[i] + addition
            spare = spare - addition
    return np.array(holding)


def gaussian(stream_key, dims, deviation, most, pieces=(), kind=jnp.bfloat16):
    entries = deviation * jax.random.normal(stream_key, dims, jnp.float32)
    if pieces:
        entries = entries * steps_of(stream_key, dims, pieces, -0.22, 0.18)
    return jnp.clip(entries, -most, most).astype(kind)


def setup_inputs(seed: int = 0, part: int = 0) -> dict:
    arg_keys = jax.random.split(jax.random.key(seed), 9)
    own_keys = jax.random.split(jax.random.fold_in(arg_keys[8], part), 9)
    tokens = gaussian(own_keys[0], (TOKENS, D), 1.0, 6.0, ((0, 16),))
    expert_ids_keys = jax.random.split(jax.random.fold_in(own_keys[1], 1), TOKENS // TOK_DEV)
    expert_ids_turns = jax.random.permutation(jax.random.fold_in(own_keys[1], 3), TOKENS // TOK_DEV)
    expert_ids = jax.vmap(lambda own, number: routed_block(jax.random.fold_in(own_keys[1], 2), own, number, TOK_DEV, EXPERTS, TOPK, CAP, 2))(expert_ids_keys, expert_ids_turns).reshape((TOKENS, TOPK))
    gate_weights = jnp.clip(0.099609375 + 0.40039062 * jax.random.uniform(own_keys[2], (TOKENS, TOPK), jnp.float32) ** steps_of(own_keys[2], (TOKENS, TOPK), ((0, 16),), -0.2, 0.2), 0.099609375, 0.5).astype(jnp.bfloat16)
    mix_coef = jnp.clip(jax.random.uniform(arg_keys[3], (EXPERTS, 2, BASES), jnp.float32, -0.5, 0.5) * steps_of(arg_keys[3], (EXPERTS, 2, BASES), ((0, 4),), -0.4, 0.0), -0.5, 0.5)
    factor_in = gaussian(arg_keys[4], (EXPERTS, 2, D, RANK), D ** -0.5, 0.09375, ((0, 16),))
    factor_out = gaussian(arg_keys[5], (EXPERTS, FF, RANK), FF ** -0.5, 0.21875, ((0, 16),))
    basis_in = gaussian(arg_keys[6], (BASES, RANK, 2 * FF), RANK ** -0.5, 0.375, ((2, 4),))
    basis_out = gaussian(arg_keys[7], (BASES, RANK, D), RANK ** -0.5, 0.375, ((2, 4),))
    return {"tokens": tokens, "expert_ids": expert_ids, "gate_weights": gate_weights, "mix_coef": mix_coef, "factor_in": factor_in, "factor_out": factor_out, "basis_in": basis_in, "basis_out": basis_out}


def reference(tokens, expert_ids, gate_weights, mix_coef, factor_in, factor_out, basis_in, basis_out):
    flat_ids = expert_ids.reshape(-1).astype(jnp.int32)
    flat_gates = gate_weights.reshape(-1).astype(jnp.float32)
    token_of = (jnp.arange(flat_ids.shape[0], dtype=jnp.int32) // TOPK).astype(jnp.int32)
    bound = EXPERTS * CAP
    basis_in32 = basis_in.astype(jnp.float32)
    basis_out32 = basis_out.astype(jnp.float32)

    def one_expert(carry, expert):
        mix_in = jnp.einsum("j,jrc->rc", mix_coef[expert, 0], basis_in32, precision=lax.Precision.HIGHEST).astype(jnp.bfloat16)
        mix_out = jnp.einsum("j,jrc->rc", mix_coef[expert, 1], basis_out32, precision=lax.Precision.HIGHEST).astype(jnp.bfloat16)
        w_gate = jnp.dot(factor_in[expert, 0], mix_in[:, :FF], preferred_element_type=jnp.float32).astype(jnp.bfloat16)
        w_up = jnp.dot(factor_in[expert, 1], mix_in[:, FF:], preferred_element_type=jnp.float32).astype(jnp.bfloat16)
        w_down = jnp.dot(factor_out[expert], mix_out, preferred_element_type=jnp.float32).astype(jnp.bfloat16)
        chosen = flat_ids == expert
        picks = jnp.nonzero(chosen, size=bound, fill_value=0)[0].astype(jnp.int32)
        valid = (jnp.arange(bound, dtype=jnp.int32) < jnp.sum(chosen.astype(jnp.int32))).astype(jnp.float32)
        owners = token_of[picks]
        rows = tokens[owners]
        gate = jnp.dot(rows, w_gate, preferred_element_type=jnp.float32)
        upper = jnp.dot(rows, w_up, preferred_element_type=jnp.float32)
        hidden = (jax.nn.silu(gate) * upper).astype(jnp.bfloat16)
        result = jnp.dot(hidden, w_down, preferred_element_type=jnp.float32).astype(jnp.bfloat16)
        weight = flat_gates[picks] * valid
        carry = carry.at[owners].add(result.astype(jnp.float32) * weight[:, None])
        return carry, None

    start = jnp.zeros(tokens.shape, jnp.float32)
    total, _ = lax.scan(one_expert, start, jnp.arange(EXPERTS, dtype=jnp.int32))
    return total.astype(jnp.bfloat16)
```

```python
import jax
import jax.numpy as jnp
from jax import lax
from jax.sharding import PartitionSpec as P


def shards(tokens, expert_ids, gate_weights, mix_coef, factor_in, factor_out, basis_in, basis_out):
    tok_count, width = tokens.shape
    hidden_units = factor_out.shape[1]
    bases, rank, col_width = basis_out.shape
    count_ep = lax.axis_size("ep")
    count_col = lax.axis_size("col")
    experts = count_ep * count_col
    me = lax.axis_index("ep") * count_col + lax.axis_index("col")
    group_rows = count_col * tok_count
    onehot = expert_ids[:, :, None] == jnp.arange(experts, dtype=jnp.int32)[None, None, :]
    dense = jnp.sum(
        jnp.where(onehot, gate_weights.astype(jnp.float32)[:, :, None], 0.0), axis=1
    ).astype(jnp.bfloat16)
    dense_all = lax.all_gather(dense, ("ep", "col"), axis=0, tiled=True)
    coef_all = lax.all_gather(mix_coef[:, 1, :], "ep", axis=0, tiled=True)
    rows = lax.all_gather(tokens, ("ep", "col"), axis=0, tiled=True)
    span_in = jnp.einsum(
        "ej,jrc->erc",
        mix_coef[:, 0, :],
        basis_in.astype(jnp.float32),
        precision=lax.Precision.HIGHEST,
    ).astype(jnp.bfloat16)
    mix_in = lax.all_to_all(span_in, "col", split_axis=0, concat_axis=2, tiled=True)[0]
    low_gate = jnp.dot(rows, factor_in[0, 0], preferred_element_type=jnp.float32).astype(
        jnp.bfloat16
    )
    low_up = jnp.dot(rows, factor_in[0, 1], preferred_element_type=jnp.float32).astype(jnp.bfloat16)
    gate = jnp.dot(low_gate, mix_in[:, :hidden_units], preferred_element_type=jnp.float32)
    upper = jnp.dot(low_up, mix_in[:, hidden_units:], preferred_element_type=jnp.float32)
    hidden = (jax.nn.silu(gate) * upper).astype(jnp.bfloat16)
    low_out = jnp.dot(hidden, factor_out[0], preferred_element_type=jnp.float32)
    weight = lax.dynamic_slice_in_dim(dense_all, me, 1, axis=1).astype(jnp.float32)
    low_out = (low_out * weight).astype(jnp.bfloat16)
    low_out = low_out.reshape(count_ep, group_rows, rank)
    swapped = lax.all_to_all(low_out, "ep", split_axis=0, concat_axis=0, tiled=True)
    every = lax.all_gather(swapped, "col", axis=1)
    every = every.reshape(experts, group_rows, rank)
    spread = jnp.einsum("ej,etr->tjr", coef_all, every.astype(jnp.float32), precision=lax.Precision.HIGHEST)
    spread = spread.astype(jnp.bfloat16).reshape(group_rows, bases * rank)
    block = jnp.dot(
        spread, basis_out.reshape(bases * rank, col_width), preferred_element_type=jnp.float32
    ).astype(jnp.bfloat16)
    return lax.all_to_all(block, "col", split_axis=0, concat_axis=1, tiled=True)


def solution(mesh):
    return jax.shard_map(
        shards,
        mesh=mesh,
        in_specs=(
            P(("groups", "ep", "col"), None),
            P(("groups", "ep", "col"), None),
            P(("groups", "ep", "col"), None),
            P("ep", None, None),
            P(("ep", "col"), None, None, None),
            P(("ep", "col"), None, None),
            P(None, None, "col"),
            P(None, None, "col"),
        ),
        out_specs=P(("groups", "ep", "col"), None),
        check_vma=False,
    )
```

```python
import functools

import jax
import jax.numpy as jnp
from jax import lax
from jax.experimental import pallas as pl
from jax.experimental.pallas import tpu as pltpu
from jax.sharding import PartitionSpec as P

F32, BF16 = jnp.float32, jnp.bfloat16


def dot(a, b):
    return jnp.dot(a, b, preferred_element_type=F32)


def fused(
    E, C, ids_ref, gates_ref, coef_smem, coef_vmem, tok_ref, fin_hbm, fout_hbm, bin_hbm, bout_hbm,
    out_ref,
    xall, fin, fout, bin_, bout, mstage, mix, call, call_s, low, zstage, zall, spread, ostage, oall,
    load_sem, coef_s_sem, s_left, s_right, s_y, s_sib, x_recv, m_send, m_recv, g_send, g_recv,
    c_send, c_recv, z_send, z_recv, o_send, o_recv,
):
    g, i, c = lax.axis_index("groups"), lax.axis_index("ep"), lax.axis_index("col")
    T, D = tok_ref.shape
    H, W = mix.shape[2], mix.shape[3]
    OW = oall.shape[2]
    R = low.shape[3]
    J = bin_.shape[0]
    hidden_units = fout.shape[0]
    i_y = (i + 2) % E
    i_s = (i // 2) * 2 + (i + 1) % 2
    i_d = (i_s + 2) % E
    me = i * C + c

    def remote(src, dst, ss, rs, dev):
        return pltpu.make_async_remote_copy(
            src_ref=src, dst_ref=dst, send_sem=ss, recv_sem=rs, device_id=dev,
            device_id_type=pl.DeviceIdType.MESH,
        )

    loads = [
        pltpu.make_async_copy(bin_hbm.at[:, pl.ds(pl.multiple_of(g * H, H), H), :], bin_, load_sem.at[0]),
        pltpu.make_async_copy(fin_hbm.at[0], fin, load_sem.at[1]),
        pltpu.make_async_copy(fout_hbm.at[0], fout, load_sem.at[2]),
        pltpu.make_async_copy(bout_hbm, bout, load_sem.at[3]),
    ]
    for ld in loads:
        ld.start()

    barrier = pltpu.get_barrier_semaphore()
    for k in range(1, E * C):
        o = (me + k) % (E * C)
        pl.semaphore_signal(barrier, inc=1, device_id=(g, o // C, o % C), device_id_type=pl.DeviceIdType.MESH)
    pl.semaphore_signal(barrier, inc=1, device_id=(1 - g, i, c), device_id_type=pl.DeviceIdType.MESH)

    xall[i, c, :, :D] = tok_ref[...]
    lane = lax.broadcasted_iota(jnp.int32, (T, 128), 1)
    table = jnp.zeros((T, 128), F32)
    for k in range(ids_ref.shape[1]):
        table += jnp.where(lane == ids_ref[:, k : k + 1], gates_ref[:, k : k + 1].astype(F32), 0.0)
    xall[i, c, :, D:] = table.astype(BF16)
    call[i] = jnp.zeros((8, 128), F32)
    call[i, :C, :J] = coef_vmem[:, 1, :]
    pl.semaphore_wait(barrier, E * C)

    def right(line_c):
        blk = xall.at[i, line_c]
        return remote(blk, blk, s_right.at[line_c], x_recv.at[i, line_c], (g, i, c + 1))

    def left(line_c):
        blk = xall.at[i, line_c]
        return remote(blk, blk, s_left.at[line_c], x_recv.at[i, line_c], (g, i, c - 1))

    def over(line_c):
        blk = xall.at[i, line_c]
        return remote(blk, blk, s_y.at[line_c], x_recv.at[i, line_c], (g, i_y, c))

    def sib(which, line_c):
        line = i if which == 0 else i_y
        blk = xall.at[line, line_c]
        return remote(blk, blk, s_sib.at[which, line_c], x_recv.at[line, line_c], (g, i_s, c))

    def arrive(line, line_c):
        blk = xall.at[line, line_c]
        remote(blk, blk, s_y.at[0], x_recv.at[line, line_c], (g, i_y, c)).wait_recv()

    @pl.when(c < C - 1)
    def _():
        right(c).start()

    @pl.when(c > 0)
    def _():
        left(c).start()

    over(c).start()
    sib(0, c).start()
    coefs = []
    for k in range(1, E):
        o = (i + k) % E
        cp = remote(call.at[i], call.at[i], c_send.at[k], c_recv.at[i], (g, o, c))
        cp.start()
        coefs.append(cp)

    loads[0].wait()
    CH = 16

    def mixing(step, carry):
        rows = pl.ds(pl.multiple_of(step * CH, CH), CH)
        acc = [None] * C
        for j in range(J):
            b = bin_[j, rows, :].astype(F32)
            for e in range(C):
                v = coef_smem[e, 0, j] * b
                acc[e] = v if acc[e] is None else acc[e] + v
        for e in range(C):
            mstage[e, rows, :] = acc[e].astype(BF16)
        return carry

    lax.fori_loop(0, H // CH, mixing, 0)

    def mix_to(dest):
        return remote(mstage.at[dest], mix.at[g, c], m_send.at[dest], m_recv.at[c], (g, i, dest))

    def mix_from(src):
        return remote(mstage.at[c], mix.at[g, src], m_send.at[c], m_recv.at[src], (g, i, src))

    def mix_cross(src):
        return remote(mix.at[g, src], mix.at[g, src], g_send.at[src], g_recv.at[src], (1 - g, i, c))

    for d in range(C - 1, 0, -1):
        @pl.when(c - d >= 0)
        def _():
            mix_to(c - d).start()

        @pl.when(c + d < C)
        def _():
            mix_to(c + d).start()

    mix[g, c] = mstage[c]
    mix_cross(c).start()

    def arrive_b(d):
        for s in ((0,) if d == 0 else (-d, d)):
            src = c + s

            @pl.when((src >= 0) & (src < C))
            def _():
                arrive(i_y, src)
                sib(1, src).start()

    for d in range(1, C):
        @pl.when(c - d >= 0)
        def _():
            arrive(i, c - d)

            @pl.when(c < C - 1)
            def _():
                right(c - d).start()

            over(c - d).start()
            sib(0, c - d).start()

        @pl.when(c + d < C)
        def _():
            arrive(i, c + d)

            @pl.when(c > 0)
            def _():
                left(c + d).start()

            over(c + d).start()
            sib(0, c + d).start()

        arrive_b(d - 1)
        for s in (-d, d):
            src = c + s

            @pl.when((src >= 0) & (src < C))
            def _():
                mix_from(src).wait_recv()
                mix_cross(src).start()

    loads[1].wait()

    def project(line):
        rows = xall[line].reshape(C * T, D + 128)[:, :D]
        low[line, 0] = dot(rows, fin[0]).astype(BF16)
        low[line, 1] = dot(rows, fin[1]).astype(BF16)

    project(i)
    arrive_b(C - 1)
    for k in range(C):
        arrive(i_s, k)
    for k in range(C):
        arrive(i_d, k)
    lax.fori_loop(1, E, lambda k, carry: (project((i + k) % E), carry)[1], 0)
    for k in range(C):
        remote(mix.at[g, k], mix.at[1 - g, k], g_send.at[k], g_recv.at[k], (1 - g, i, c)).wait_recv()
    loads[2].wait()

    wide = lax.broadcasted_iota(jnp.int32, (C * T, 128), 1)

    def expert(k, carry):
        line = (i + k) % E
        parts = []
        for b in range(C // 2):
            mg = jnp.concatenate([mix[0, b], mix[1, b]], axis=0)
            mu = jnp.concatenate([mix[0, C // 2 + b], mix[1, C // 2 + b]], axis=0)
            gate = dot(low[line, 0], mg)
            upper = dot(low[line, 1], mu)
            parts.append((gate / (1.0 + jnp.exp(-gate)) * upper).astype(BF16))
        hidden = jnp.concatenate(parts, axis=1)
        z = dot(hidden, fout[...])
        table = xall[line].reshape(C * T, D + 128)[:, D:].astype(F32)
        weight = jnp.sum(jnp.where(wide == me, table, 0.0), axis=1, keepdims=True)
        zstage[line] = (z * weight).astype(BF16)
        return carry

    def z_to(line, dest):
        return remote(zstage.at[line], zall.at[me], z_send.at[line, dest], z_recv.at[me], (g, line, dest))

    for k in list(range(1, E)) + [0]:
        line = (i + k) % E
        expert(k, 0)
        for m in range(C):
            dest = (c + m) % C
            if k or m:
                z_to(line, dest).start()
    zall[me] = zstage[i]

    for k in range(1, E):
        o = (i + k) % E
        remote(call.at[o], call.at[o], c_send.at[k], c_recv.at[o], (g, o, c)).wait_recv()
    cc = pltpu.make_async_copy(call, call_s, coef_s_sem)
    cc.start()
    cc.wait()
    loads[3].wait()
    for k in range(1, E * C):
        o = (me + k) % (E * C)
        remote(zstage.at[i], zall.at[o], z_send.at[i, c], z_recv.at[o], (g, o // C, o % C)).wait_recv()

    for col in range(R // 128):
        lanes = slice(col * 128, (col + 1) * 128)

        def combine(step, carry):
            rows = pl.ds(pl.multiple_of(step * 16, 16), 16)
            z = [zall[e, rows, lanes].astype(F32) for e in range(E * C)]
            for j in range(J):
                acc = call_s[0, 0, j] * z[0]
                for e in range(1, E * C):
                    acc = acc + call_s[e // C, e % C, j] * z[e]
                spread[rows, j * R + col * 128 : j * R + (col + 1) * 128] = acc.astype(BF16)
            return carry

        lax.fori_loop(0, C * T // 16, combine, 0)

    step_w = 256
    for n in range(OW // step_w):
        cols = slice(n * step_w, (n + 1) * step_w)
        block = dot(spread[...], bout[:, cols]).astype(BF16)
        ostage[:, :, cols] = block.reshape(C, T, step_w)

    def o_to(dest):
        return remote(ostage.at[dest], oall.at[c], o_send.at[dest], o_recv.at[c], (g, i, dest))

    for k in range(1, C):
        o_to((c + k) % C).start()
    oall[c] = ostage[c]
    for k in range(1, C):
        o = (c + k) % C
        remote(ostage.at[o], oall.at[o], o_send.at[o], o_recv.at[o], (g, i, o)).wait_recv()
    for k in range(C):
        out_ref[:, k * OW : (k + 1) * OW] = oall[k]

    for k in range(C):
        @pl.when((c < C - 1) & (k <= c))
        def _():
            right(k).wait_send()

        @pl.when((c > 0) & (k >= c))
        def _():
            left(k).wait_send()

        over(k).wait_send()
        sib(0, k).wait_send()
        sib(1, k).wait_send()
        mix_cross(k).wait_send()
    for cp in coefs:
        cp.wait_send()
    for k in range(1, C):
        mix_to((c + k) % C).wait_send()
        o_to((c + k) % C).wait_send()
    for k in range(E):
        for m in range(C):
            if k or m:
                z_to((i + k) % E, (c + m) % C).wait_send()


def shards_kernel(E, C, tokens, expert_ids, gate_weights, mix_coef, factor_in, factor_out, basis_in, basis_out):
    T, D = tokens.shape
    J, R, W = basis_in.shape
    OW = basis_out.shape[2]
    FFU = factor_out.shape[1]
    H = R // 2
    vm = pl.BlockSpec(memory_space=pltpu.VMEM)
    anym = pl.BlockSpec(memory_space=pl.ANY)
    dma = pltpu.SemaphoreType.DMA
    return pl.pallas_call(
        functools.partial(fused, E, C),
        out_shape=jax.ShapeDtypeStruct((T, D), BF16),
        in_specs=[vm, vm, pl.BlockSpec(memory_space=pltpu.SMEM), vm, vm, anym, anym, anym, anym],
        out_specs=vm,
        scratch_shapes=[
            pltpu.VMEM((E, C, T, D + 128), BF16),
            pltpu.VMEM((2, D, R), BF16),
            pltpu.VMEM((FFU, R), BF16),
            pltpu.VMEM((J, H, W), BF16),
            pltpu.VMEM((J * R, OW), BF16),
            pltpu.VMEM((C, H, W), BF16),
            pltpu.VMEM((2, C, H, W), BF16),
            pltpu.VMEM((E, 8, 128), F32),
            pltpu.SMEM((E, 8, 128), F32),
            pltpu.VMEM((E, 2, C * T, R), BF16),
            pltpu.VMEM((E, C * T, R), BF16),
            pltpu.VMEM((E * C, C * T, R), BF16),
            pltpu.VMEM((C * T, J * R), BF16),
            pltpu.VMEM((C, T, OW), BF16),
            pltpu.VMEM((C, T, OW), BF16),
            dma((4,)), dma, dma((C,)), dma((C,)), dma((C,)), dma((2, C)), dma((E, C)),
            dma((C,)), dma((C,)), dma((C,)), dma((C,)),
            dma((E,)), dma((E,)), dma((E, C)), dma((E * C,)), dma((C,)), dma((C,)),
        ],
        compiler_params=pltpu.CompilerParams(
            collective_id=0, has_side_effects=True, vmem_limit_bytes=48 * 1024 * 1024
        ),
    )(
        expert_ids, gate_weights, mix_coef, mix_coef, tokens, factor_in, factor_out, basis_in,
        basis_out.reshape(J * R, OW),
    )


def shards(tokens, expert_ids, gate_weights, mix_coef, factor_in, factor_out, basis_in, basis_out):
    tok_count, width = tokens.shape
    hidden_units = factor_out.shape[1]
    bases, rank, col_width = basis_out.shape
    count_ep = lax.axis_size("ep")
    count_col = lax.axis_size("col")
    experts = count_ep * count_col
    me = lax.axis_index("ep") * count_col + lax.axis_index("col")
    group_rows = count_col * tok_count
    onehot = expert_ids[:, :, None] == jnp.arange(experts, dtype=jnp.int32)[None, None, :]
    dense = jnp.sum(
        jnp.where(onehot, gate_weights.astype(jnp.float32)[:, :, None], 0.0), axis=1
    ).astype(jnp.bfloat16)
    dense_all = lax.all_gather(dense, ("ep", "col"), axis=0, tiled=True)
    coef_all = lax.all_gather(mix_coef[:, 1, :], "ep", axis=0, tiled=True)
    rows = lax.all_gather(tokens, ("ep", "col"), axis=0, tiled=True)
    span_in = jnp.einsum(
        "ej,jrc->erc",
        mix_coef[:, 0, :],
        basis_in.astype(jnp.float32),
        precision=lax.Precision.HIGHEST,
    ).astype(jnp.bfloat16)
    mix_in = lax.all_to_all(span_in, "col", split_axis=0, concat_axis=2, tiled=True)[0]
    low_gate = jnp.dot(rows, factor_in[0, 0], preferred_element_type=jnp.float32).astype(
        jnp.bfloat16
    )
    low_up = jnp.dot(rows, factor_in[0, 1], preferred_element_type=jnp.float32).astype(jnp.bfloat16)
    gate = jnp.dot(low_gate, mix_in[:, :hidden_units], preferred_element_type=jnp.float32)
    upper = jnp.dot(low_up, mix_in[:, hidden_units:], preferred_element_type=jnp.float32)
    hidden = (jax.nn.silu(gate) * upper).astype(jnp.bfloat16)
    low_out = jnp.dot(hidden, factor_out[0], preferred_element_type=jnp.float32)
    weight = lax.dynamic_slice_in_dim(dense_all, me, 1, axis=1).astype(jnp.float32)
    low_out = (low_out * weight).astype(jnp.bfloat16)
    low_out = low_out.reshape(count_ep, group_rows, rank)
    swapped = lax.all_to_all(low_out, "ep", split_axis=0, concat_axis=0, tiled=True)
    every = lax.all_gather(swapped, "col", axis=1)
    every = every.reshape(experts, group_rows, rank)
    spread = jnp.einsum("ej,etr->tjr", coef_all, every.astype(jnp.float32), precision=lax.Precision.HIGHEST)
    spread = spread.astype(jnp.bfloat16).reshape(group_rows, bases * rank)
    block = jnp.dot(
        spread, basis_out.reshape(bases * rank, col_width), preferred_element_type=jnp.float32
    ).astype(jnp.bfloat16)
    return lax.all_to_all(block, "col", split_axis=0, concat_axis=1, tiled=True)


def solution(mesh):
    E, C = mesh.shape["ep"], mesh.shape["col"]
    small = E == 4 and C == 4 and mesh.shape["groups"] == 2
    return jax.shard_map(
        functools.partial(shards_kernel, E, C) if small else shards,
        mesh=mesh,
        in_specs=(
            P(("groups", "ep", "col"), None),
            P(("groups", "ep", "col"), None),
            P(("groups", "ep", "col"), None),
            P("ep", None, None),
            P(("ep", "col"), None, None, None),
            P(("ep", "col"), None, None),
            P(None, None, "col"),
            P(None, None, "col"),
        ),
        out_specs=P(("groups", "ep", "col"), None),
        check_vma=False,
    )
```

```python
import functools

import jax
import jax.numpy as jnp
from jax import lax
from jax.experimental import pallas as pl
from jax.experimental.pallas import tpu as pltpu
from jax.sharding import PartitionSpec as P

F32, BF16 = jnp.float32, jnp.bfloat16


def dot(a, b):
    return jnp.dot(a, b, preferred_element_type=F32)


def fused(
    E, C, ids_hbm, gates_hbm, coef_hbm, tok_hbm, fin_hbm, fout_hbm, bin_hbm, bout_hbm,
    out_ref,
    ids_ref, gates_ref, coef_smem, coef_vmem, xall, fin, fout, bin_, bout, mstage, mix, call, call_s, low, zstage, zall, spread, ostage, oall,
    small_sem, load_sem, coef_s_sem, s_left, s_right, s_y, s_sib, x_recv, m_send, m_recv, g_send, g_recv,
    c_send, c_recv, z_send, z_recv, o_send, o_recv,
):
    g, i, c = lax.axis_index("groups"), lax.axis_index("ep"), lax.axis_index("col")
    T, D = tok_hbm.shape
    H, W = mix.shape[2], mix.shape[3]
    OW = bout.shape[1]
    R = low.shape[3]
    J = bin_.shape[0]
    hidden_units = fout.shape[0]
    i_y = (i + 2) % E
    i_s = (i // 2) * 2 + (i + 1) % 2
    i_d = (i_s + 2) % E
    me = i * C + c

    def remote(src, dst, ss, rs, dev):
        return pltpu.make_async_remote_copy(
            src_ref=src, dst_ref=dst, send_sem=ss, recv_sem=rs, device_id=dev,
            device_id_type=pl.DeviceIdType.MESH,
        )

    small = [
        pltpu.make_async_copy(ids_hbm, ids_ref, small_sem.at[0]),
        pltpu.make_async_copy(gates_hbm, gates_ref, small_sem.at[1]),
        pltpu.make_async_copy(coef_hbm, coef_vmem, small_sem.at[2]),
        pltpu.make_async_copy(coef_hbm, coef_smem, small_sem.at[3]),
        pltpu.make_async_copy(tok_hbm, xall.at[i, c, :, pl.ds(0, D)], small_sem.at[4]),
    ]
    for ld in small:
        ld.start()
    loads = [
        pltpu.make_async_copy(bin_hbm.at[:, pl.ds(pl.multiple_of(g * H, H), H), :], bin_, load_sem.at[0]),
        pltpu.make_async_copy(fin_hbm.at[0], fin, load_sem.at[1]),
        pltpu.make_async_copy(fout_hbm.at[0], fout, load_sem.at[2]),
        pltpu.make_async_copy(bout_hbm, bout, load_sem.at[3]),
    ]
    loads[0].start()

    barrier = pltpu.get_barrier_semaphore()
    for k in range(1, E * C):
        o = (me + k) % (E * C)
        pl.semaphore_signal(barrier, inc=1, device_id=(g, o // C, o % C), device_id_type=pl.DeviceIdType.MESH)
    pl.semaphore_signal(barrier, inc=1, device_id=(1 - g, i, c), device_id_type=pl.DeviceIdType.MESH)

    for ld in small:
        ld.wait()
    number = lax.broadcasted_iota(jnp.int32, (128, T), 0)
    table = jnp.zeros((128, T), F32)
    for k in range(ids_ref.shape[0]):
        table += jnp.where(number == ids_ref[k : k + 1, :], gates_ref[k : k + 1, :].astype(F32), 0.0)
    xall[i, c, :, D:] = table.T.astype(BF16)
    call[i] = jnp.zeros((8, 128), F32)
    call[i, :C, :J] = coef_vmem[:, 1, :]
    pl.semaphore_wait(barrier, E * C)

    parts_x = ((0, D // 2), (D // 2, D // 2 + 128))

    def piece(line, line_c, p):
        return xall.at[line, line_c, :, pl.ds(*parts_x[p])]

    def right(line_c, p):
        blk = piece(i, line_c, p)
        return remote(blk, blk, s_right.at[line_c, p], x_recv.at[i, line_c, p], (g, i, c + 1))

    def left(line_c, p):
        blk = piece(i, line_c, p)
        return remote(blk, blk, s_left.at[line_c, p], x_recv.at[i, line_c, p], (g, i, c - 1))

    def over(line_c, p):
        blk = piece(i, line_c, p)
        return remote(blk, blk, s_y.at[line_c, p], x_recv.at[i, line_c, p], (g, i_y, c))

    def sib(which, line_c, p):
        line = i if which == 0 else i_y
        blk = piece(line, line_c, p)
        return remote(blk, blk, s_sib.at[which, line_c, p], x_recv.at[line, line_c, p], (g, i_s, c))

    def arrive(line, line_c, p):
        blk = piece(line, line_c, p)
        remote(blk, blk, s_y.at[0, p], x_recv.at[line, line_c, p], (g, i_y, c)).wait_recv()

    for p in range(2):
        @pl.when(c < C - 1)
        def _():
            right(c, p).start()

        @pl.when(c > 0)
        def _():
            left(c, p).start()

        over(c, p).start()
        sib(0, c, p).start()
    coefs = []
    for k in range(1, E):
        o = (i + k) % E
        cp = remote(call.at[i], call.at[i], c_send.at[k], c_recv.at[i], (g, o, c))
        cp.start()
        coefs.append(cp)

    loads[0].wait()
    for ld in loads[1:]:
        ld.start()
    CH = 16

    def mixing(step, carry):
        rows = pl.ds(pl.multiple_of(step * CH, CH), CH)
        acc = [None] * C
        for j in range(J):
            b = bin_[j, rows, :].astype(F32)
            for e in range(C):
                v = coef_smem[e, 0, j] * b
                acc[e] = v if acc[e] is None else acc[e] + v
        for e in range(C):
            mstage[e, rows, :] = acc[e].astype(BF16)
        return carry

    lax.fori_loop(0, H // CH, mixing, 0)

    def mix_to(dest):
        return remote(mstage.at[dest], mix.at[g, c], m_send.at[dest], m_recv.at[c], (g, i, dest))

    def mix_from(src):
        return remote(mstage.at[c], mix.at[g, src], m_send.at[c], m_recv.at[src], (g, i, src))

    def mix_cross(src):
        return remote(mix.at[g, src], mix.at[g, src], g_send.at[src], g_recv.at[src], (1 - g, i, c))

    def mix_start(d):
        for s in (-d, d):
            dest = c + s

            @pl.when((dest >= 0) & (dest < C))
            def _():
                mix_to(dest).start()

    def mix_pass(d):
        for s in (-d, d):
            src = c + s

            @pl.when((src >= 0) & (src < C))
            def _():
                mix_from(src).wait_recv()
                mix_cross(src).start()

    mix_start(1)
    mix[g, c] = mstage[c]
    mix_cross(c).start()

    def arrive_b(d):
        for p in range(2):
            for s in ((0,) if d == 0 else (-d, d)):
                src = c + s

                @pl.when((src >= 0) & (src < C))
                def _():
                    arrive(i_y, src, p)
                    sib(1, src, p).start()

    for d in range(1, C):
        for p in range(2):
            @pl.when(c - d >= 0)
            def _():
                arrive(i, c - d, p)

                @pl.when(c < C - 1)
                def _():
                    right(c - d, p).start()

                over(c - d, p).start()
                sib(0, c - d, p).start()

            @pl.when(c + d < C)
            def _():
                arrive(i, c + d, p)

                @pl.when(c > 0)
                def _():
                    left(c + d, p).start()

                over(c + d, p).start()
                sib(0, c + d, p).start()

        if d < C - 1:
            mix_start(d + 1)
        arrive_b(d - 1)
        if d > 1:
            mix_pass(d - 1)

    arrive_b(C - 1)
    mix_pass(C - 1)

    loads[1].wait()

    def project(line):
        rows = xall[line].reshape(C * T, D + 128)[:, :D]
        low[line, 0] = dot(rows, fin[0]).astype(BF16)
        low[line, 1] = dot(rows, fin[1]).astype(BF16)

    project(i)
    for k in range(C):
        for p in range(2):
            arrive(i_s, k, p)
            arrive(i_d, k, p)
    lax.fori_loop(1, E, lambda k, carry: (project((i + k) % E), carry)[1], 0)
    for k in range(C):
        remote(mix.at[g, k], mix.at[1 - g, k], g_send.at[k], g_recv.at[k], (1 - g, i, c)).wait_recv()
    loads[2].wait()

    wide = lax.broadcasted_iota(jnp.int32, (C * T, 128), 1)

    def expert(k, carry):
        line = (i + k) % E
        parts = []
        for b in range(C // 2):
            mg = jnp.concatenate([mix[0, b], mix[1, b]], axis=0)
            mu = jnp.concatenate([mix[0, C // 2 + b], mix[1, C // 2 + b]], axis=0)
            gate = dot(low[line, 0], mg)
            upper = dot(low[line, 1], mu)
            parts.append((gate / (1.0 + jnp.exp(-gate)) * upper).astype(BF16))
        hidden = jnp.concatenate(parts, axis=1)
        z = dot(hidden, fout[...])
        table = xall[line].reshape(C * T, D + 128)[:, D:].astype(F32)
        weight = jnp.sum(jnp.where(wide == me, table, 0.0), axis=1, keepdims=True)
        zstage[line] = (z * weight).astype(BF16)
        return carry

    def z_to(line, dest):
        return remote(zstage.at[line], zall.at[me], z_send.at[line, dest], z_recv.at[me], (g, line, dest))

    for k in list(range(1, E)) + [0]:
        line = (i + k) % E
        expert(k, 0)
        for m in range(C - 1, -1, -1):
            for s in ((0,) if m == 0 else (-m, m)):
                if k == 0 and m == 0:
                    continue
                dest = c + s

                @pl.when((dest >= 0) & (dest < C))
                def _():
                    z_to(line, dest).start()
    zall[me] = zstage[i]

    for k in range(1, E):
        o = (i + k) % E
        remote(call.at[o], call.at[o], c_send.at[k], c_recv.at[o], (g, o, c)).wait_recv()
    cc = pltpu.make_async_copy(call, call_s, coef_s_sem)
    cc.start()
    cc.wait()
    loads[3].wait()
    for k in range(1, E * C):
        o = (me + k) % (E * C)
        remote(zstage.at[i], zall.at[o], z_send.at[i, c], z_recv.at[o], (g, o // C, o % C)).wait_recv()

    for col in range(R // 128):
        lanes = slice(col * 128, (col + 1) * 128)

        def combine(step, carry):
            rows = pl.ds(pl.multiple_of(step * 16, 16), 16)
            z = [zall[e, rows, lanes].astype(F32) for e in range(E * C)]
            for j in range(J):
                acc = call_s[0, 0, j] * z[0]
                for e in range(1, E * C):
                    acc = acc + call_s[e // C, e % C, j] * z[e]
                spread[rows, j * R + col * 128 : j * R + (col + 1) * 128] = acc.astype(BF16)
            return carry

        lax.fori_loop(0, C * T // 16, combine, 0)

    steps = o_send.shape[1]
    step_w = OW // steps

    def o_copy(n, dest, src):
        return remote(ostage.at[n, dest], oall.at[n, src], o_send.at[dest, n], o_recv.at[src, n], (g, i, dest))

    for n in range(steps):
        block = dot(spread[...], bout[:, n * step_w : (n + 1) * step_w]).astype(BF16)
        ostage[n] = block.reshape(C, T, step_w)
        for k in range(1, C):
            o_copy(n, (c + k) % C, c).start()
        oall[n, c] = ostage[n, c]
    for n in range(steps):
        for k in range(1, C):
            o_copy(n, (c + k) % C, (c + k) % C).wait_recv()
        for k in range(C):
            out_ref[:, k * OW + n * step_w : k * OW + (n + 1) * step_w] = oall[n, k]

    for k in range(C):
        for p in range(2):
            @pl.when((c < C - 1) & (k <= c))
            def _():
                right(k, p).wait_send()

            @pl.when((c > 0) & (k >= c))
            def _():
                left(k, p).wait_send()

            over(k, p).wait_send()
            sib(0, k, p).wait_send()
            sib(1, k, p).wait_send()
        mix_cross(k).wait_send()
    for cp in coefs:
        cp.wait_send()
    for k in range(1, C):
        mix_to((c + k) % C).wait_send()
        for n in range(steps):
            o_copy(n, (c + k) % C, c).wait_send()
    for k in range(E):
        for m in range(C):
            if k or m:
                z_to((i + k) % E, (c + m) % C).wait_send()


def shards_kernel(E, C, tokens, expert_ids, gate_weights, mix_coef, factor_in, factor_out, basis_in, basis_out):
    T, D = tokens.shape
    J, R, W = basis_in.shape
    OW = basis_out.shape[2]
    FFU = factor_out.shape[1]
    H = R // 2
    vm = pl.BlockSpec(memory_space=pltpu.VMEM)
    anym = pl.BlockSpec(memory_space=pl.ANY)
    dma = pltpu.SemaphoreType.DMA
    return pl.pallas_call(
        functools.partial(fused, E, C),
        out_shape=jax.ShapeDtypeStruct((T, D), BF16),
        in_specs=[anym] * 8,
        out_specs=vm,
        scratch_shapes=[
            pltpu.VMEM((expert_ids.shape[1], T), jnp.int32),
            pltpu.VMEM((expert_ids.shape[1], T), BF16),
            pltpu.SMEM(mix_coef.shape, F32),
            pltpu.VMEM(mix_coef.shape, F32),
            pltpu.VMEM((E, C, T, D + 128), BF16),
            pltpu.VMEM((2, D, R), BF16),
            pltpu.VMEM((FFU, R), BF16),
            pltpu.VMEM((J, H, W), BF16),
            pltpu.VMEM((J * R, OW), BF16),
            pltpu.VMEM((C, H, W), BF16),
            pltpu.VMEM((2, C, H, W), BF16),
            pltpu.VMEM((E, 8, 128), F32),
            pltpu.SMEM((E, 8, 128), F32),
            pltpu.VMEM((E, 2, C * T, R), BF16),
            pltpu.VMEM((E, C * T, R), BF16),
            pltpu.VMEM((E * C, C * T, R), BF16),
            pltpu.VMEM((C * T, J * R), BF16),
            pltpu.VMEM((4, C, T, OW // 4), BF16),
            pltpu.VMEM((4, C, T, OW // 4), BF16),
            dma((5,)), dma((4,)), dma, dma((C, 2)), dma((C, 2)), dma((C, 2)), dma((2, C, 2)), dma((E, C, 2)),
            dma((C,)), dma((C,)), dma((C,)), dma((C,)),
            dma((E,)), dma((E,)), dma((E, C)), dma((E * C,)), dma((C, 4)), dma((C, 4)),
        ],
        compiler_params=pltpu.CompilerParams(
            collective_id=0, has_side_effects=True, vmem_limit_bytes=62 * 1024 * 1024
        ),
    )(
        expert_ids.T, gate_weights.T, mix_coef, tokens, factor_in, factor_out, basis_in,
        basis_out.reshape(J * R, OW),
    )


def shards(tokens, expert_ids, gate_weights, mix_coef, factor_in, factor_out, basis_in, basis_out):
    tok_count, width = tokens.shape
    hidden_units = factor_out.shape[1]
    bases, rank, col_width = basis_out.shape
    count_ep = lax.axis_size("ep")
    count_col = lax.axis_size("col")
    experts = count_ep * count_col
    me = lax.axis_index("ep") * count_col + lax.axis_index("col")
    group_rows = count_col * tok_count
    onehot = expert_ids[:, :, None] == jnp.arange(experts, dtype=jnp.int32)[None, None, :]
    dense = jnp.sum(
        jnp.where(onehot, gate_weights.astype(jnp.float32)[:, :, None], 0.0), axis=1
    ).astype(jnp.bfloat16)
    dense_all = lax.all_gather(dense, ("ep", "col"), axis=0, tiled=True)
    coef_all = lax.all_gather(mix_coef[:, 1, :], "ep", axis=0, tiled=True)
    rows = lax.all_gather(tokens, ("ep", "col"), axis=0, tiled=True)
    span_in = jnp.einsum(
        "ej,jrc->erc",
        mix_coef[:, 0, :],
        basis_in.astype(jnp.float32),
        precision=lax.Precision.HIGHEST,
    ).astype(jnp.bfloat16)
    mix_in = lax.all_to_all(span_in, "col", split_axis=0, concat_axis=2, tiled=True)[0]
    low_gate = jnp.dot(rows, factor_in[0, 0], preferred_element_type=jnp.float32).astype(
        jnp.bfloat16
    )
    low_up = jnp.dot(rows, factor_in[0, 1], preferred_element_type=jnp.float32).astype(jnp.bfloat16)
    gate = jnp.dot(low_gate, mix_in[:, :hidden_units], preferred_element_type=jnp.float32)
    upper = jnp.dot(low_up, mix_in[:, hidden_units:], preferred_element_type=jnp.float32)
    hidden = (jax.nn.silu(gate) * upper).astype(jnp.bfloat16)
    low_out = jnp.dot(hidden, factor_out[0], preferred_element_type=jnp.float32)
    weight = lax.dynamic_slice_in_dim(dense_all, me, 1, axis=1).astype(jnp.float32)
    low_out = (low_out * weight).astype(jnp.bfloat16)
    low_out = low_out.reshape(count_ep, group_rows, rank)
    swapped = lax.all_to_all(low_out, "ep", split_axis=0, concat_axis=0, tiled=True)
    every = lax.all_gather(swapped, "col", axis=1)
    every = every.reshape(experts, group_rows, rank)
    spread = jnp.einsum("ej,etr->tjr", coef_all, every.astype(jnp.float32), precision=lax.Precision.HIGHEST)
    spread = spread.astype(jnp.bfloat16).reshape(group_rows, bases * rank)
    block = jnp.dot(
        spread, basis_out.reshape(bases * rank, col_width), preferred_element_type=jnp.float32
    ).astype(jnp.bfloat16)
    return lax.all_to_all(block, "col", split_axis=0, concat_axis=1, tiled=True)


def solution(mesh):
    E, C = mesh.shape["ep"], mesh.shape["col"]
    small = E == 4 and C == 4 and mesh.shape["groups"] == 2
    return jax.shard_map(
        functools.partial(shards_kernel, E, C) if small else shards,
        mesh=mesh,
        in_specs=(
            P(("groups", "ep", "col"), None),
            P(("groups", "ep", "col"), None),
            P(("groups", "ep", "col"), None),
            P("ep", None, None),
            P(("ep", "col"), None, None, None),
            P(("ep", "col"), None, None),
            P(None, None, "col"),
            P(None, None, "col"),
        ),
        out_specs=P(("groups", "ep", "col"), None),
        check_vma=False,
    )
```

```python
import functools

import jax
import jax.numpy as jnp
from jax import lax
from jax.experimental import pallas as pl
from jax.experimental.pallas import tpu as pltpu
from jax.sharding import PartitionSpec as P

F32, BF16 = jnp.float32, jnp.bfloat16


def dot(a, b):
    return jnp.dot(a, b, preferred_element_type=F32)


def fused(
    E, C, ids_hbm, gates_hbm, coef_hbm, tok_hbm, fin_hbm, fout_hbm, bin_hbm, bout_hbm,
    out_ref,
    ids_ref, gates_ref, coef_smem, coef_vmem, xall, fin, fout, bin_, bout, mstage, mix, call, call_s, low, zstage, zall, spread, ostage, oall,
    small_sem, load_sem, coef_s_sem, s_left, s_right, s_y, s_sib, x_recv, m_send, m_recv, g_send, g_recv,
    c_send, c_recv, z_send, z_recv, o_send, o_recv,
):
    g, i, c = lax.axis_index("groups"), lax.axis_index("ep"), lax.axis_index("col")
    T, D = tok_hbm.shape
    H, W = mix.shape[2], mix.shape[3]
    OW = bout.shape[1]
    R = low.shape[3]
    J = bin_.shape[0]
    hidden_units = fout.shape[0]
    i_y = (i + 2) % E
    i_s = (i // 2) * 2 + (i + 1) % 2
    i_d = (i_s + 2) % E
    me = i * C + c

    def remote(src, dst, ss, rs, dev):
        return pltpu.make_async_remote_copy(
            src_ref=src, dst_ref=dst, send_sem=ss, recv_sem=rs, device_id=dev,
            device_id_type=pl.DeviceIdType.MESH,
        )

    small = [
        pltpu.make_async_copy(ids_hbm, ids_ref, small_sem.at[0]),
        pltpu.make_async_copy(gates_hbm, gates_ref, small_sem.at[1]),
        pltpu.make_async_copy(coef_hbm, coef_vmem, small_sem.at[2]),
        pltpu.make_async_copy(coef_hbm, coef_smem, small_sem.at[3]),
        pltpu.make_async_copy(tok_hbm, xall.at[i, c, :, pl.ds(0, D)], small_sem.at[4]),
    ]
    for ld in small:
        ld.start()
    loads = [
        pltpu.make_async_copy(bin_hbm.at[:, pl.ds(pl.multiple_of(g * H, H), H), :], bin_, load_sem.at[0]),
        pltpu.make_async_copy(fin_hbm.at[0], fin, load_sem.at[1]),
        pltpu.make_async_copy(fout_hbm.at[0], fout, load_sem.at[2]),
        pltpu.make_async_copy(bout_hbm, bout, load_sem.at[3]),
    ]
    loads[0].start()

    barrier = pltpu.get_barrier_semaphore()
    for k in range(1, E * C):
        o = (me + k) % (E * C)
        pl.semaphore_signal(barrier, inc=1, device_id=(g, o // C, o % C), device_id_type=pl.DeviceIdType.MESH)
    pl.semaphore_signal(barrier, inc=1, device_id=(1 - g, i, c), device_id_type=pl.DeviceIdType.MESH)

    for ld in small:
        ld.wait()
    number = lax.broadcasted_iota(jnp.int32, (128, T), 0)
    table = jnp.zeros((128, T), F32)
    for k in range(ids_ref.shape[0]):
        table += jnp.where(number == ids_ref[k : k + 1, :], gates_ref[k : k + 1, :].astype(F32), 0.0)
    xall[i, c, :, D:] = table.T.astype(BF16)
    call[i] = jnp.zeros((8, 128), F32)
    call[i, :C, :J] = coef_vmem[:, 1, :]
    pl.semaphore_wait(barrier, E * C)

    parts_x = ((0, D // 2), (D // 2, D // 2 + 128))

    def piece(line, line_c, p):
        return xall.at[line, line_c, :, pl.ds(*parts_x[p])]

    def right(line_c, p):
        blk = piece(i, line_c, p)
        return remote(blk, blk, s_right.at[line_c, p], x_recv.at[i, line_c, p], (g, i, c + 1))

    def left(line_c, p):
        blk = piece(i, line_c, p)
        return remote(blk, blk, s_left.at[line_c, p], x_recv.at[i, line_c, p], (g, i, c - 1))

    def over(line_c, p):
        blk = piece(i, line_c, p)
        return remote(blk, blk, s_y.at[line_c, p], x_recv.at[i, line_c, p], (g, i_y, c))

    def sib(which, line_c, p):
        line = i if which == 0 else i_y
        blk = piece(line, line_c, p)
        return remote(blk, blk, s_sib.at[which, line_c, p], x_recv.at[line, line_c, p], (g, i_s, c))

    def arrive(line, line_c, p):
        blk = piece(line, line_c, p)
        remote(blk, blk, s_y.at[0, p], x_recv.at[line, line_c, p], (g, i_y, c)).wait_recv()

    for p in range(2):
        @pl.when(c < C - 1)
        def _():
            right(c, p).start()

        @pl.when(c > 0)
        def _():
            left(c, p).start()

        over(c, p).start()
        sib(0, c, p).start()
    coefs = []
    for k in range(1, E):
        o = (i + k) % E
        cp = remote(call.at[i], call.at[i], c_send.at[k], c_recv.at[i], (g, o, c))
        cp.start()
        coefs.append(cp)

    loads[0].wait()
    for ld in loads[1:]:
        ld.start()
    CH = 16

    def mixing(step, carry):
        rows = pl.ds(pl.multiple_of(step * CH, CH), CH)
        acc = [None] * C
        for j in range(J):
            b = bin_[j, rows, :].astype(F32)
            for e in range(C):
                v = coef_smem[e, 0, j] * b
                acc[e] = v if acc[e] is None else acc[e] + v
        for e in range(C):
            mstage[e, rows, :] = acc[e].astype(BF16)
        return carry

    lax.fori_loop(0, H // CH, mixing, 0)

    def mix_to(dest):
        return remote(mstage.at[dest], mix.at[g, c], m_send.at[dest], m_recv.at[c], (g, i, dest))

    def mix_from(src):
        return remote(mstage.at[c], mix.at[g, src], m_send.at[c], m_recv.at[src], (g, i, src))

    def mix_cross(src):
        return remote(mix.at[g, src], mix.at[g, src], g_send.at[src], g_recv.at[src], (1 - g, i, c))

    def mix_start(d):
        for s in (-d, d):
            dest = c + s

            @pl.when((dest >= 0) & (dest < C))
            def _():
                mix_to(dest).start()

    def mix_pass(d):
        for s in (-d, d):
            src = c + s

            @pl.when((src >= 0) & (src < C))
            def _():
                mix_from(src).wait_recv()
                mix_cross(src).start()

    mix_start(1)
    mix[g, c] = mstage[c]
    mix_cross(c).start()

    def arrive_b(d):
        for p in range(2):
            for s in ((0,) if d == 0 else (-d, d)):
                src = c + s

                @pl.when((src >= 0) & (src < C))
                def _():
                    arrive(i_y, src, p)
                    sib(1, src, p).start()

    for d in range(1, C):
        for p in range(2):
            @pl.when(c - d >= 0)
            def _():
                arrive(i, c - d, p)

                @pl.when(c < C - 1)
                def _():
                    right(c - d, p).start()

                over(c - d, p).start()
                sib(0, c - d, p).start()

            @pl.when(c + d < C)
            def _():
                arrive(i, c + d, p)

                @pl.when(c > 0)
                def _():
                    left(c + d, p).start()

                over(c + d, p).start()
                sib(0, c + d, p).start()

        if d < C - 1:
            mix_start(d + 1)
        arrive_b(d - 1)
        if d > 1:
            mix_pass(d - 1)

    arrive_b(C - 1)
    mix_pass(C - 1)

    loads[1].wait()

    def project(line):
        rows = xall[line].reshape(C * T, D + 128)[:, :D]
        low[line, 0] = dot(rows, fin[0]).astype(BF16)
        low[line, 1] = dot(rows, fin[1]).astype(BF16)

    project(i)
    project(i_y)
    for line in (i_s, i_d):
        for k in range(C):
            for p in range(2):
                arrive(line, k, p)
        project(line)
    for k in range(C):
        remote(mix.at[g, k], mix.at[1 - g, k], g_send.at[k], g_recv.at[k], (1 - g, i, c)).wait_recv()
    loads[2].wait()

    wide = lax.broadcasted_iota(jnp.int32, (C * T, 128), 1)

    def expert(k, carry):
        line = (i + k) % E
        parts = []
        for b in range(C // 2):
            mg = jnp.concatenate([mix[0, b], mix[1, b]], axis=0)
            mu = jnp.concatenate([mix[0, C // 2 + b], mix[1, C // 2 + b]], axis=0)
            gate = dot(low[line, 0], mg)
            upper = dot(low[line, 1], mu)
            parts.append((gate / (1.0 + jnp.exp(-gate)) * upper).astype(BF16))
        hidden = jnp.concatenate(parts, axis=1)
        z = dot(hidden, fout[...])
        table = xall[line].reshape(C * T, D + 128)[:, D:].astype(F32)
        weight = jnp.sum(jnp.where(wide == me, table, 0.0), axis=1, keepdims=True)
        zstage[line] = (z * weight).astype(BF16)
        return carry

    def z_to(line, dest):
        return remote(zstage.at[line], zall.at[me], z_send.at[line, dest], z_recv.at[me], (g, line, dest))

    for k in list(range(1, E)) + [0]:
        line = (i + k) % E
        expert(k, 0)
        for m in range(C - 1, -1, -1):
            for s in ((0,) if m == 0 else (-m, m)):
                if k == 0 and m == 0:
                    continue
                dest = c + s

                @pl.when((dest >= 0) & (dest < C))
                def _():
                    z_to(line, dest).start()
    zall[me] = zstage[i]

    for k in range(1, E):
        o = (i + k) % E
        remote(call.at[o], call.at[o], c_send.at[k], c_recv.at[o], (g, o, c)).wait_recv()
    cc = pltpu.make_async_copy(call, call_s, coef_s_sem)
    cc.start()
    cc.wait()
    loads[3].wait()
    for k in range(1, E * C):
        o = (me + k) % (E * C)
        remote(zstage.at[i], zall.at[o], z_send.at[i, c], z_recv.at[o], (g, o // C, o % C)).wait_recv()

    for col in range(R // 128):
        lanes = slice(col * 128, (col + 1) * 128)

        def combine(step, carry):
            rows = pl.ds(pl.multiple_of(step * 16, 16), 16)
            z = [zall[e, rows, lanes].astype(F32) for e in range(E * C)]
            for j in range(J):
                acc = call_s[0, 0, j] * z[0]
                for e in range(1, E * C):
                    acc = acc + call_s[e // C, e % C, j] * z[e]
                spread[rows, j * R + col * 128 : j * R + (col + 1) * 128] = acc.astype(BF16)
            return carry

        lax.fori_loop(0, C * T // 16, combine, 0)

    steps = o_send.shape[1]
    step_w = OW // steps

    def o_copy(n, dest, src):
        return remote(ostage.at[n, dest], oall.at[n, src], o_send.at[dest, n], o_recv.at[src, n], (g, i, dest))

    for n in range(steps):
        block = dot(spread[...], bout[:, n * step_w : (n + 1) * step_w]).astype(BF16)
        ostage[n] = block.reshape(C, T, step_w)
        for k in range(1, C):
            o_copy(n, (c + k) % C, c).start()
        oall[n, c] = ostage[n, c]
    for n in range(steps):
        for k in range(1, C):
            o_copy(n, (c + k) % C, (c + k) % C).wait_recv()
        for k in range(C):
            out_ref[:, k * OW + n * step_w : k * OW + (n + 1) * step_w] = oall[n, k]

    for k in range(C):
        for p in range(2):
            @pl.when((c < C - 1) & (k <= c))
            def _():
                right(k, p).wait_send()

            @pl.when((c > 0) & (k >= c))
            def _():
                left(k, p).wait_send()

            over(k, p).wait_send()
            sib(0, k, p).wait_send()
            sib(1, k, p).wait_send()
        mix_cross(k).wait_send()
    for cp in coefs:
        cp.wait_send()
    for k in range(1, C):
        mix_to((c + k) % C).wait_send()
        for n in range(steps):
            o_copy(n, (c + k) % C, c).wait_send()
    for k in range(E):
        for m in range(C):
            if k or m:
                z_to((i + k) % E, (c + m) % C).wait_send()


def shards_kernel(E, C, tokens, expert_ids, gate_weights, mix_coef, factor_in, factor_out, basis_in, basis_out):
    T, D = tokens.shape
    J, R, W = basis_in.shape
    OW = basis_out.shape[2]
    FFU = factor_out.shape[1]
    H = R // 2
    vm = pl.BlockSpec(memory_space=pltpu.VMEM)
    anym = pl.BlockSpec(memory_space=pl.ANY)
    dma = pltpu.SemaphoreType.DMA
    return pl.pallas_call(
        functools.partial(fused, E, C),
        out_shape=jax.ShapeDtypeStruct((T, D), BF16),
        in_specs=[anym] * 8,
        out_specs=vm,
        scratch_shapes=[
            pltpu.VMEM((expert_ids.shape[1], T), jnp.int32),
            pltpu.VMEM((expert_ids.shape[1], T), BF16),
            pltpu.SMEM(mix_coef.shape, F32),
            pltpu.VMEM(mix_coef.shape, F32),
            pltpu.VMEM((E, C, T, D + 128), BF16),
            pltpu.VMEM((2, D, R), BF16),
            pltpu.VMEM((FFU, R), BF16),
            pltpu.VMEM((J, H, W), BF16),
            pltpu.VMEM((J * R, OW), BF16),
            pltpu.VMEM((C, H, W), BF16),
            pltpu.VMEM((2, C, H, W), BF16),
            pltpu.VMEM((E, 8, 128), F32),
            pltpu.SMEM((E, 8, 128), F32),
            pltpu.VMEM((E, 2, C * T, R), BF16),
            pltpu.VMEM((E, C * T, R), BF16),
            pltpu.VMEM((E * C, C * T, R), BF16),
            pltpu.VMEM((C * T, J * R), BF16),
            pltpu.VMEM((4, C, T, OW // 4), BF16),
            pltpu.VMEM((4, C, T, OW // 4), BF16),
            dma((5,)), dma((4,)), dma, dma((C, 2)), dma((C, 2)), dma((C, 2)), dma((2, C, 2)), dma((E, C, 2)),
            dma((C,)), dma((C,)), dma((C,)), dma((C,)),
            dma((E,)), dma((E,)), dma((E, C)), dma((E * C,)), dma((C, 4)), dma((C, 4)),
        ],
        compiler_params=pltpu.CompilerParams(
            collective_id=0, has_side_effects=True, vmem_limit_bytes=62 * 1024 * 1024
        ),
    )(
        expert_ids.T, gate_weights.T, mix_coef, tokens, factor_in, factor_out, basis_in,
        basis_out.reshape(J * R, OW),
    )


def shards(tokens, expert_ids, gate_weights, mix_coef, factor_in, factor_out, basis_in, basis_out):
    tok_count, width = tokens.shape
    hidden_units = factor_out.shape[1]
    bases, rank, col_width = basis_out.shape
    count_ep = lax.axis_size("ep")
    count_col = lax.axis_size("col")
    experts = count_ep * count_col
    me = lax.axis_index("ep") * count_col + lax.axis_index("col")
    group_rows = count_col * tok_count
    onehot = expert_ids[:, :, None] == jnp.arange(experts, dtype=jnp.int32)[None, None, :]
    dense = jnp.sum(
        jnp.where(onehot, gate_weights.astype(jnp.float32)[:, :, None], 0.0), axis=1
    ).astype(jnp.bfloat16)
    dense_all = lax.all_gather(dense, ("ep", "col"), axis=0, tiled=True)
    coef_all = lax.all_gather(mix_coef[:, 1, :], "ep", axis=0, tiled=True)
    rows = lax.all_gather(tokens, ("ep", "col"), axis=0, tiled=True)
    span_in = jnp.einsum(
        "ej,jrc->erc",
        mix_coef[:, 0, :],
        basis_in.astype(jnp.float32),
        precision=lax.Precision.HIGHEST,
    ).astype(jnp.bfloat16)
    mix_in = lax.all_to_all(span_in, "col", split_axis=0, concat_axis=2, tiled=True)[0]
    low_gate = jnp.dot(rows, factor_in[0, 0], preferred_element_type=jnp.float32).astype(
        jnp.bfloat16
    )
    low_up = jnp.dot(rows, factor_in[0, 1], preferred_element_type=jnp.float32).astype(jnp.bfloat16)
    gate = jnp.dot(low_gate, mix_in[:, :hidden_units], preferred_element_type=jnp.float32)
    upper = jnp.dot(low_up, mix_in[:, hidden_units:], preferred_element_type=jnp.float32)
    hidden = (jax.nn.silu(gate) * upper).astype(jnp.bfloat16)
    low_out = jnp.dot(hidden, factor_out[0], preferred_element_type=jnp.float32)
    weight = lax.dynamic_slice_in_dim(dense_all, me, 1, axis=1).astype(jnp.float32)
    low_out = (low_out * weight).astype(jnp.bfloat16)
    low_out = low_out.reshape(count_ep, group_rows, rank)
    swapped = lax.all_to_all(low_out, "ep", split_axis=0, concat_axis=0, tiled=True)
    every = lax.all_gather(swapped, "col", axis=1)
    every = every.reshape(experts, group_rows, rank)
    spread = jnp.einsum("ej,etr->tjr", coef_all, every.astype(jnp.float32), precision=lax.Precision.HIGHEST)
    spread = spread.astype(jnp.bfloat16).reshape(group_rows, bases * rank)
    block = jnp.dot(
        spread, basis_out.reshape(bases * rank, col_width), preferred_element_type=jnp.float32
    ).astype(jnp.bfloat16)
    return lax.all_to_all(block, "col", split_axis=0, concat_axis=1, tiled=True)


def solution(mesh):
    E, C = mesh.shape["ep"], mesh.shape["col"]
    small = E == 4 and C == 4 and mesh.shape["groups"] == 2
    return jax.shard_map(
        functools.partial(shards_kernel, E, C) if small else shards,
        mesh=mesh,
        in_specs=(
            P(("groups", "ep", "col"), None),
            P(("groups", "ep", "col"), None),
            P(("groups", "ep", "col"), None),
            P("ep", None, None),
            P(("ep", "col"), None, None, None),
            P(("ep", "col"), None, None),
            P(None, None, "col"),
            P(None, None, "col"),
        ),
        out_specs=P(("groups", "ep", "col"), None),
        check_vma=False,
    )
```
